32 devices in a mesh: groups: 2 (over y), seq: 4 (over z), head: 4 (over x, core).
Axes of the slice: x: 2, y: 2, z: 4, core: 2. Of those that a mesh axis runs over, the one named last changes fastest.
Arguments:
- tokens: bfloat16 [2048, 4096], P(('groups', 'seq'), 'head'), parts along dimension 0, may hold values from -6 to 6
- norm_gain: float32 [4096], replicated, may hold values from 0.1 to 1.9
- w_query: bfloat16 [4096, 4096], P('seq', 'head'), may hold values from -0.09375 to 0.09375
- w_key: bfloat16 [4096, 4096], P('seq', 'head'), may hold values from -0.1875 to 0.1875
- w_value: bfloat16 [4096, 4096], P('seq', 'head'), may hold values from -0.09375 to 0.09375
- w_out: bfloat16 [4096, 4096], P('seq', 'head'), may hold values from -0.375 to 0.375
- database: bfloat16 [64, 128, 4096], P(('groups', 'seq'), None, 'head'), parts along dimension 0, may hold values from -6 to 6
- nbr_shard: int32 [32, 2], P(('groups', 'seq')), parts along dimension 0, may hold values from 0 to 3, all different within a row; in each aligned block of 4 rows (0 to 3, 4 to 7, ...) at most 4 rows name the same one
- nbr_row: int32 [32, 2], P(('groups', 'seq')), parts along dimension 0, may hold values from 0 to 7
Outputs:
- attended: bfloat16 [2048, 4096], P(('groups', 'seq'), 'head'), parts along dimension 0
The draws below stay inside these ranges and needn't reach their ends.
There are 2 independent parts, one for each index of `groups`. The reference program is written for one: setup_inputs(seed, part) draws one part's arguments, and reference() takes and returns one part's arrays. A program takes and returns all parts, laid end to end along the dimension named above; an argument that names none is the same for every part. Nothing has to cross between parts.
Inputs may be any that keep to these rules, and one draw needn't show every extreme that they name: `nbr_shard`: each span's two neighbours come from two different shards. Among the 4 spans of one index of seq, no shard is named more than 4 times, a bound that some block reaches.
All inputs are finite; a program needn't handle non-finite values.
Results may differ from the reference program's by a relative error of at most 0.012.
Values may be sent and summed in bfloat16 or wider, within the bound.
A program may use at most 128 MiB of HBM per device.

```python
import math
import jax
import jax.numpy as jnp
import numpy as np
from jax import lax

D = 4096
HEADS = 32
HD = 128
SPAN = 64
NTOK = 128
CH_DEV = 4
ROWS_DEV = 8
SPANS = 16
TOKENS = 1024
DB_ROWS = 32
CAP = 4
N_SEQ = 4


def plant(entries, own_key, smallest, largest):
    longest = entries.shape.index(max(entries.shape))
    spots = []
    for shift in (0, 1):
        where = [jax.random.randint(jax.random.fold_in(own_key, axis), (), 0, length) for axis, length in enumerate(entries.shape)]
        where[longest] = (where[longest] + shift) % entries.shape[longest]
        spots.append(tuple(where))
    return entries.at[spots[0]].set(smallest).at[spots[1]].set(largest)


def steps_of(rng, extent, split, least, top_value):
    gain = 1.0
    for axis_at, shards_of in split:
        steps = jax.random.uniform(jax.random.fold_in(jax.random.fold_in(rng, 6), axis_at), (shards_of,), jnp.float32, least / len(split), top_value / len(split))
        gain = gain * jnp.repeat(jnp.exp(steps), extent[axis_at] // shards_of).reshape((-1,) + (1,) * (len(extent) - 1 - axis_at))
    return gain


def cumulative_ranks(number_of, slope):
    portions = [(1 << 20) // math.isqrt(grade ** slope) + 1 for grade in range(1, number_of + 1)]
    spread = 1 + sum(portions) // (1 << 30)
    return np.cumsum(np.array([max(1, weight // spread) for weight in portions]))


def ranked_ids(own_key, extent, number_of, slope):
    grid = cumulative_ranks(number_of, slope)
    pick = jax.random.randint(jax.random.fold_in(own_key, 1), extent, 0, int(grid[number_of - 1]))
    rank = jnp.searchsorted(jnp.asarray(grid, jnp.int32), pick, side="right")
    return jax.random.permutation(jax.random.fold_in(own_key, 2), number_of)[rank].astype(jnp.int32)


def routed_block(own_key, own, number, rows, amount, top, bound, lean):
    sequence = jax.random.permutation(own_key, amount)
    crowded, usual = load_shares(amount, rows * top, bound, lean, True), load_shares(amount, rows * top, bound, lean, False)
    places = jnp.arange(amount)

    def named(sizes, turn):
        used = int((sizes > 0).sum())
        fixed = max(1, used // 4)
        moved = fixed + (places - fixed + turn * (used - fixed)) % max(1, amount - fixed)
        return jnp.zeros((amount,), jnp.int32).at[sequence[jnp.where(places < fixed, places, moved)]].set(jnp.asarray(sizes, jnp.int32))

    sizes = jnp.where(number % 4 == 0, named(crowded, number // 4), named(usual, number - number // 4 - 1))
    mixed = jax.random.permutation(jax.random.fold_in(own, 3), amount)
    source_of, taker = mixed[0:amount // 2 * 2:2], mixed[1:amount // 2 * 2:2]
    margin = jnp.minimum(sizes[source_of] - 1, bound - sizes[taker]) // 2
    margin = jnp.where((source_of == sequence[0]) | (taker == sequence[0]) | (sizes[taker] == 0), 0, jnp.maximum(margin, 0))
    moved = jax.random.randint(jax.random.fold_in(own, 4), (amount // 2,), 0, 1 << 20) % (margin + 1)
    sizes = sizes.at[source_of].add(-moved).at[taker].add(moved)
    members = jnp.searchsorted(jnp.cumsum(sizes), jnp.arange(rows * top), side="right").astype(jnp.int32)
    grid = members.reshape(top, rows).T
    grid = grid[jax.random.permutation(jax.random.fold_in(own, 1), rows)]
    turn = jax.random.randint(jax.random.fold_in(own, 2), (rows, 1), 0, top)
    return jnp.take_along_axis(grid, (jnp.arange(top)[None, :] + turn) % top, axis=1)


def load_shares(number_of, total, most, slope, full):
    weights = [(1 << 20) // math.isqrt(grade ** slope) + 1 for grade in range(1, number_of + 1)]
    largest = most if full else min(most, max(-(-total // number_of), total * weights[0] // sum(weights)))
    least = 1 if total - largest >= number_of - 1 else 0
    counts, rest = [largest] + [least] * (number_of - 1), total - largest - least * (number_of - 1)
    while rest > 0:
        movable = [i for i in range(1, number_of) if counts[i] < largest] or [i for i in range(1, number_of) if counts[i] < most]
        mass, remaining = sum([weights[i] for i in movable]), rest
        for i in movable:
            extra = min(most - counts[i], max(1, remaining * weights[i] // mass), rest)
            counts[i] = counts[i] + extra
            rest = rest - extra
    return np.array(counts)


def scatter_about(own_key, extent, width, most, shards=(), dtype=jnp.bfloat16):
    drawn = jax.random.normal(own_key, extent, jnp.float32) * width
    if len(shards) > 0:
        drawn = steps_of(own_key, extent, shards, -0.22, 0.18) * drawn
    return jnp.clip(drawn, min=-most, max=most).astype(dtype)


def setup_inputs(seed: int = 0, part: int = 0) -> dict:
    streams_of = jax.random.split(jax.random.key(seed), 10)
    part_keys = jax.random.split(jax.random.fold_in(streams_of[9], part), 10)
    tokens = scatter_about(part_keys[0], (TOKENS, D), 1.0, 6.0, ((0, 4), (1, 4)))
    norm_gain = jnp.clip(1.0 + 0.18 * jax.random.normal(streams_of[1], (D,), jnp.float32), 0.1, 1.9)
    w_query = scatter_about(streams_of[2], (D, D), D ** -0.5, 0.09375, ((0, 4), (1, 4)))
    w_key = scatter_about(streams_of[3], (D, D), (D // 4) ** -0.5, 0.1875, ((0, 4), (1, 4)))
    w_value = scatter_about(streams_of[4], (D, D), D ** -0.5, 0.09375, ((0, 4), (1, 4)))
    w_out = scatter_about(streams_of[5], (D, D), (D // 16) ** -0.5, 0.375, ((0, 4), (1, 4)))
    database = scatter_about(part_keys[6], (DB_ROWS, NTOK, D), 1.0, 6.0, ((0, 4), (2, 4)))
    nbr_shard_keys = jax.random.split(jax.random.fold_in(part_keys[7], 1), SPANS // CH_DEV)
    nbr_shard_turns = jax.random.permutation(jax.random.fold_in(part_keys[7], 3), SPANS // CH_DEV)
    nbr_shard = jax.vmap(lambda own, number: routed_block(jax.random.fold_in(part_keys[7], 2), own, number, CH_DEV, N_SEQ, 2, CAP, 2))(nbr_shard_keys, nbr_shard_turns).reshape((SPANS, 2))
    nbr_row = plant(ranked_ids(part_keys[8], (SPANS, 2), ROWS_DEV, 2), jax.random.fold_in(part_keys[8], 3), 0, ROWS_DEV - 1).astype(jnp.int32)
    return {"tokens": tokens, "norm_gain": norm_gain, "w_query": w_query, "w_key": w_key, "w_value": w_value, "w_out": w_out, "database": database, "nbr_shard": nbr_shard, "nbr_row": nbr_row}


def reference(tokens, norm_gain, w_query, w_key, w_value, w_out, database, nbr_shard, nbr_row):
    x = tokens.astype(jnp.float32)
    inverse = lax.rsqrt(lax.optimization_barrier(jnp.mean(x * x, axis=-1, keepdims=True)) + 1e-06)
    normed = (x * inverse * norm_gain.astype(jnp.float32)).astype(jnp.bfloat16)
    query = (jnp.dot(normed, w_query, preferred_element_type=jnp.float32) / jnp.sqrt(jnp.float32(HD))).astype(jnp.bfloat16)
    index = (nbr_shard * ROWS_DEV + nbr_row).reshape(-1).astype(jnp.int32)
    neighbours = jnp.take(database, index, axis=0).reshape(-1, D)
    keys = jnp.dot(neighbours, w_key, preferred_element_type=jnp.float32).astype(jnp.bfloat16)
    values = jnp.dot(neighbours, w_value, preferred_element_type=jnp.float32).astype(jnp.bfloat16)
    qh = query.reshape(SPANS, SPAN, HEADS, HD).astype(jnp.float32)
    kh = keys.reshape(SPANS, 2 * NTOK, HEADS, HD).astype(jnp.float32)
    vh = values.reshape(SPANS, 2 * NTOK, HEADS, HD).astype(jnp.float32)
    scores = jnp.einsum('cqhd,ckhd->chqk', qh, kh)
    weights = jax.nn.softmax(scores, axis=-1).astype(jnp.bfloat16)
    context = jnp.einsum('chqk,ckhd->cqhd', weights.astype(jnp.float32), vh).astype(jnp.bfloat16)
    context = context.reshape(TOKENS, D)
    return jnp.dot(context, w_out, preferred_element_type=jnp.float32).astype(jnp.bfloat16)
```

```python
import jax
import jax.numpy as jnp
from jax import lax
from jax.sharding import PartitionSpec as P

HD = 128


def gather_rows(weight):
    parts = lax.axis_size("groups")
    rows = weight.shape[0] // parts
    half = lax.dynamic_slice_in_dim(weight, lax.axis_index("groups") * rows, rows, axis=0)
    return lax.all_gather(half, ("seq", "groups"), axis=0, tiled=True)


def local(tokens, norm_gain, w_query, w_key, w_value, w_out, database, nbr_shard, nbr_row):
    whole = lax.all_gather(tokens, "head", axis=1, tiled=True)
    x = whole.astype(jnp.float32)
    inverse = lax.rsqrt(jnp.mean(x * x, axis=-1, keepdims=True) + 1e-06)
    normed = (x * inverse * norm_gain).astype(jnp.bfloat16)
    tok_rows = normed.shape[0]
    width = w_query.shape[1]
    heads_dev = width // HD
    query = jnp.dot(
        normed,
        gather_rows(w_query),
        preferred_element_type=jnp.float32,
    )
    query = (query / jnp.sqrt(jnp.float32(HD))).astype(jnp.bfloat16)
    num_seq = lax.axis_size("seq")
    spans_dev = nbr_shard.shape[0]
    count = 2 * spans_dev
    capacity = max(2, 4 * spans_dev // num_seq)
    shard_flat = nbr_shard.reshape(-1)
    row_flat = nbr_row.reshape(-1)
    positions = jnp.arange(count, dtype=jnp.int32)
    earlier = positions[None, :] < positions[:, None]
    slot_flat = jnp.sum(earlier & (shard_flat[:, None] == shard_flat[None, :]), axis=1)
    owners = jnp.arange(num_seq, dtype=jnp.int32)
    slots = jnp.arange(capacity, dtype=jnp.int32)
    match = (shard_flat[:, None, None] == owners[None, :, None]) & (
        slot_flat[:, None, None] == slots[None, None, :]
    )
    wanted = jnp.sum(jnp.where(match, row_flat[:, None, None], 0), axis=0)
    asked = lax.all_to_all(wanted, "seq", split_axis=0, concat_axis=0, tiled=True)
    ntok = database.shape[1]
    feat_dev = database.shape[2]
    wanted_slots = shard_flat * capacity + slot_flat
    outgoing = jnp.take(database, asked.reshape(-1), axis=0)
    outgoing = outgoing.reshape(num_seq, capacity, ntok, feat_dev)
    arrived = lax.all_to_all(outgoing, "seq", split_axis=0, concat_axis=0, tiled=True)
    arrived = arrived.reshape(num_seq * capacity, ntok, feat_dev)
    picked = jnp.take(arrived, wanted_slots, axis=0)
    key_full, value_full = (
        gather_rows(w_key),
        gather_rows(w_value),
    )
    piece = lax.all_gather(picked, "head", axis=2, tiled=True)
    flat = piece.reshape(-1, piece.shape[2])
    keys = jnp.dot(flat, key_full, preferred_element_type=jnp.float32)
    values = jnp.dot(flat, value_full, preferred_element_type=jnp.float32)
    keys = keys.astype(jnp.bfloat16)
    values = values.astype(jnp.bfloat16)
    keys = keys.reshape(spans_dev, 2 * ntok, heads_dev, HD)
    values = values.reshape(spans_dev, 2 * ntok, heads_dev, HD)
    span_len = tok_rows // spans_dev
    qh = query.reshape(spans_dev, span_len, heads_dev, HD)
    scores = jnp.einsum("cqhd,ckhd->chqk", qh, keys, preferred_element_type=jnp.float32)
    weights = jax.nn.softmax(scores, axis=-1).astype(jnp.bfloat16)
    context = jnp.einsum("chqk,ckhd->cqhd", weights, values, preferred_element_type=jnp.float32)
    context = context.astype(jnp.bfloat16).reshape(tok_rows, width)
    out_full = gather_rows(w_out)
    attended = jnp.dot(
        lax.all_gather(context, "head", axis=1, tiled=True),
        out_full,
        preferred_element_type=jnp.float32,
    )
    return attended.astype(jnp.bfloat16)


def solution(mesh):
    return jax.shard_map(
        local,
        mesh=mesh,
        in_specs=(
            P(("groups", "seq"), "head"),
            P(),
            P("seq", "head"),
            P("seq", "head"),
            P("seq", "head"),
            P("seq", "head"),
            P(("groups", "seq"), None, "head"),
            P(("groups", "seq"), None),
            P(("groups", "seq"), None),
        ),
        out_specs=P(("groups", "seq"), "head"),
        check_vma=False,
    )
```

```python
import jax
import jax.numpy as jnp
from jax import lax
from jax.sharding import PartitionSpec as P

HD = 128


def column_half(weight):
    cols = weight.shape[1] // 2
    return lax.dynamic_slice_in_dim(weight, lax.axis_index("groups") * cols, cols, axis=1)


def gather_halves(weight):
    mine = lax.all_gather(column_half(weight), "seq", axis=0, tiled=True)
    other = lax.ppermute(mine, "groups", [(0, 1), (1, 0)])
    return mine, other


def project(rows, halves):
    mine, other = (jnp.dot(rows, half, preferred_element_type=jnp.float32) for half in halves)
    first = lax.axis_index("groups") == 0
    return jnp.concatenate([jnp.where(first, mine, other), jnp.where(first, other, mine)], axis=1)


def normalize(tokens, norm_gain):
    x = tokens.astype(jnp.float32)
    feat_dev = tokens.shape[1]
    total = lax.psum(jnp.sum(x * x, axis=-1, keepdims=True), "head")
    inverse = lax.rsqrt(total / (feat_dev * lax.axis_size("head")) + 1e-06)
    gain = lax.dynamic_slice_in_dim(norm_gain, lax.axis_index("head") * feat_dev, feat_dev)
    return (x * inverse * gain).astype(jnp.bfloat16)


def every_query(normed, w_query):
    scale = jnp.sqrt(jnp.float32(HD))
    num = lax.axis_size("seq")
    if num == lax.axis_size("head"):
        swap = [(a * num + b, b * num + a) for a in range(num) for b in range(num)]
        turned = lax.ppermute(normed, ("seq", "head"), swap)
        rows = lax.all_gather(turned, "head", axis=0, tiled=True)
        part = jnp.dot(rows, w_query, preferred_element_type=jnp.float32) / scale
        return lax.psum(part.astype(jnp.bfloat16), "seq")
    rows = lax.all_gather(normed, "head", axis=1, tiled=True)
    query = jnp.dot(
        rows,
        lax.all_gather(w_query, "seq", axis=0, tiled=True),
        preferred_element_type=jnp.float32,
    )
    return lax.all_gather((query / scale).astype(jnp.bfloat16), "seq", axis=0, tiled=True)


def local(tokens, norm_gain, w_query, w_key, w_value, w_out, database, nbr_shard, nbr_row):
    key_halves = gather_halves(w_key)
    value_halves = gather_halves(w_value)
    out_halves = gather_halves(w_out)
    rows_dev, ntok, _ = database.shape
    flat = lax.all_gather(database, "head", axis=2, tiled=True).reshape(rows_dev * ntok, -1)
    query = every_query(normalize(tokens, norm_gain), w_query)

    me = lax.axis_index("seq")
    near = lax.all_gather(jnp.concatenate([nbr_shard, nbr_row], axis=1), "seq", axis=0, tiled=True)
    here = near[:, :2] == me
    mine = jnp.any(here, axis=1)
    row = jnp.sum(jnp.where(here, near[:, 2:], 0), axis=1)

    spans = near.shape[0]
    width = w_key.shape[1]
    heads_dev = width // HD
    span_len = query.shape[0] // spans
    keys = project(flat, key_halves).astype(jnp.bfloat16).reshape(rows_dev, ntok, width)
    values = project(flat, value_halves).astype(jnp.bfloat16).reshape(rows_dev, ntok, width)
    keys = jnp.take(keys, row, axis=0).reshape(spans, ntok, heads_dev, HD)
    values = jnp.take(values, row, axis=0).reshape(spans, ntok, heads_dev, HD)
    qh = query.reshape(spans, span_len, heads_dev, HD)
    scores = jnp.einsum("cqhd,ckhd->chqk", qh, keys, preferred_element_type=jnp.float32)
    scores = jnp.where(mine[:, None, None, None], scores, -jnp.inf)
    top = jnp.max(scores, axis=-1)
    summed = jnp.sum(jnp.exp(scores - jnp.where(jnp.isfinite(top), top, 0.0)[..., None]), axis=-1)
    tops, sums = lax.all_gather(jnp.stack([top, summed]), "seq", axis=1)
    most = jnp.max(tops, axis=0)
    denominator = jnp.sum(jnp.exp(tops - most) * sums, axis=0)
    weights = (jnp.exp(scores - most[..., None]) / denominator[..., None]).astype(jnp.bfloat16)
    context = jnp.einsum("chqk,ckhd->cqhd", weights, values, preferred_element_type=jnp.float32)
    context = context.astype(jnp.bfloat16).reshape(spans * span_len, width)
    context = lax.psum_scatter(context, "seq", scatter_dimension=0, tiled=True)
    attended = project(lax.all_gather(context, "head", axis=1, tiled=True), out_halves)
    return attended.astype(jnp.bfloat16)


def solution(mesh):
    return jax.shard_map(
        local,
        mesh=mesh,
        in_specs=(
            P(("groups", "seq"), "head"),
            P(),
            P("seq", "head"),
            P("seq", "head"),
            P("seq", "head"),
            P("seq", "head"),
            P(("groups", "seq"), None, "head"),
            P(("groups", "seq"), None),
            P(("groups", "seq"), None),
        ),
        out_specs=P(("groups", "seq"), "head"),
        check_vma=False,
    )
```

```python
import functools

import jax
import jax.numpy as jnp
from jax import lax
from jax.experimental import pallas as pl
from jax.experimental.pallas import tpu as pltpu
from jax.sharding import PartitionSpec as P

HD = 128


def column_half(weight):
    cols = weight.shape[1] // 2
    return lax.dynamic_slice_in_dim(weight, lax.axis_index("groups") * cols, cols, axis=1)


def gather_halves(weight):
    mine = lax.all_gather(column_half(weight), "seq", axis=0, tiled=True)
    other = lax.ppermute(mine, "groups", [(0, 1), (1, 0)])
    return mine, other


def project(rows, halves):
    mine, other = (jnp.dot(rows, half, preferred_element_type=jnp.float32) for half in halves)
    first = lax.axis_index("groups") == 0
    return jnp.concatenate([jnp.where(first, mine, other), jnp.where(first, other, mine)], axis=1)


def normalize(tokens, norm_gain):
    x = tokens.astype(jnp.float32)
    feat_dev = tokens.shape[1]
    total = lax.psum(jnp.sum(x * x, axis=-1, keepdims=True), "head")
    inverse = lax.rsqrt(total / (feat_dev * lax.axis_size("head")) + 1e-06)
    gain = lax.dynamic_slice_in_dim(norm_gain, lax.axis_index("head") * feat_dev, feat_dev)
    return (x * inverse * gain).astype(jnp.bfloat16)


def partial_query(normed, w_query):
    scale = jnp.sqrt(jnp.float32(HD))
    num = lax.axis_size("seq")
    if num == lax.axis_size("head"):
        swap = [(a * num + b, b * num + a) for a in range(num) for b in range(num)]
        turned = lax.ppermute(normed, ("seq", "head"), swap)
        rows = lax.all_gather(turned, "head", axis=0, tiled=True)
        part = jnp.dot(rows, w_query, preferred_element_type=jnp.float32) / scale
        return part.astype(jnp.bfloat16)
    rows = lax.all_gather(normed, "head", axis=1, tiled=True)
    query = jnp.dot(
        rows,
        lax.all_gather(w_query, "seq", axis=0, tiled=True),
        preferred_element_type=jnp.float32,
    )
    return (query / scale).astype(jnp.bfloat16)


def whole_query(part):
    if lax.axis_size("seq") == lax.axis_size("head"):
        return lax.psum(part, "seq")
    return lax.all_gather(part, "seq", axis=0, tiled=True)


MESH = pl.DeviceIdType.MESH


def project_kernel(
    n_seq, n_head, database, w_key, w_value, keys, values, whole, held, total,
    near_send, near_recv, side_send, side_recv, row_send, row_recv, row_copy,
):
    g, z, h = lax.axis_index("groups"), lax.axis_index("seq"), lax.axis_index("head")
    weights = (w_key, w_value)
    depth, width = w_key.shape
    half = depth // 2
    feats = database.shape[1]
    tile = min(256, width)

    barrier = pltpu.get_barrier_semaphore()

    def greet(**where):
        pl.semaphore_signal(barrier, inc=1, device_id=where, device_id_type=MESH)

    @pl.when(z > 0)
    def _():
        greet(seq=z - 1)

    @pl.when(z < n_seq - 1)
    def _():
        greet(seq=z + 1)

    greet(groups=1 - g)
    for step in range(1, n_head):
        greet(head=lax.rem(h + step, n_head))

    ends = jnp.where(z > 0, 0, 1) + jnp.where(z < n_seq - 1, 0, 1)
    pl.semaphore_wait(barrier, n_head + 2 - ends)

    def span(owner, part):
        return pl.ds(pl.multiple_of(owner * depth + part * half, half), half)

    def along(w, owner, way, own=False):
        source = held.at[w, span(owner, g)]
        if own:
            source = weights[w].at[pl.ds(pl.multiple_of(g * half, half), half)]
        return pltpu.make_async_remote_copy(
            src_ref=source,
            dst_ref=held.at[w, span(owner, g)],
            send_sem=near_send.at[w, owner, way],
            recv_sem=near_recv.at[w, owner],
            device_id={"seq": z + 1 - 2 * way},
            device_id_type=MESH,
        )

    def across(w, owner, part):
        return pltpu.make_async_remote_copy(
            src_ref=held.at[w, span(owner, part)],
            dst_ref=held.at[w, span(owner, part)],
            send_sem=side_send.at[w, owner],
            recv_sem=side_recv.at[w, owner],
            device_id={"groups": 1 - g},
            device_id_type=MESH,
        )

    def columns(source):
        return pl.ds(pl.multiple_of(source * feats, feats), feats)

    def row_move(source, target):
        return pltpu.make_async_remote_copy(
            src_ref=database,
            dst_ref=whole.at[:, columns(source)],
            send_sem=row_send.at[target],
            recv_sem=row_recv.at[source],
            device_id={"head": target},
            device_id_type=MESH,
        )

    for w in range(2):

        @pl.when(z < n_seq - 1)
        def _():
            along(w, z, 0, own=True).start()

        @pl.when(z > 0)
        def _():
            along(w, z, 1, own=True).start()

    for step in range(1, n_head):
        row_move(h, lax.rem(h + step, n_head)).start()
    keep = pltpu.make_async_copy(database, whole.at[:, columns(h)], row_copy)
    keep.start()

    def valid(d, way):
        return z - d >= 0 if way == 0 else z + d < n_seq

    def owner_of(d, way):
        return z - d if way == 0 else z + d

    def forward(d):
        for w in range(2):
            for way in range(2):
                owner = owner_of(d, way)

                @pl.when(valid(d, way))
                def _():
                    along(w, owner, way).wait_recv()
                    across(w, owner, g).start()

                    @pl.when(z < n_seq - 1 if way == 0 else z > 0)
                    def _():
                        along(w, owner, way).start()

    def add(w, owner, block, first=False):
        left = whole.at[:, pl.ds(pl.multiple_of(owner * depth, depth), depth)]

        def body(t, carry):
            at = pl.ds(pl.multiple_of(t * tile, tile), tile)
            term = jnp.dot(left[...], block[:, at], preferred_element_type=jnp.float32)
            if first:
                total[w, :, at] = term
            else:
                total[w, :, at] += term
            return carry

        lax.fori_loop(0, width // tile, body, 0)

    def multiply(d):
        for w in range(2):
            for way in range(2):
                owner = owner_of(d, way)

                @pl.when(valid(d, way))
                def _():
                    across(w, owner, 1 - g).wait_recv()
                    add(w, owner, held.at[w, pl.ds(pl.multiple_of(owner * depth, depth), depth)])

    early = min(2, n_seq - 1)
    for d in range(1, early + 1):
        forward(d)
    keep.wait()
    for step in range(1, n_head):
        source = lax.rem(h + step, n_head)
        row_move(source, source).wait_recv()
    for w in range(2):
        add(w, z, weights[w], first=True)
    for d in range(1, n_seq):
        if d > early:
            forward(d)
        if d < n_seq - 1:
            multiply(d)
    if n_seq > 1:
        multiply(n_seq - 1)

    keys[...] = total[0].astype(keys.dtype)
    values[...] = total[1].astype(values.dtype)

    for step in range(1, n_head):
        row_move(h, lax.rem(h + step, n_head)).wait_send()
    for w in range(2):

        @pl.when(z < n_seq - 1)
        def _():
            along(w, z, 0, own=True).wait_send()

        @pl.when(z > 0)
        def _():
            along(w, z, 1, own=True).wait_send()

        for d in range(1, n_seq):
            for way in range(2):
                owner = owner_of(d, way)

                @pl.when(valid(d, way))
                def _():
                    across(w, owner, g).wait_send()

                    @pl.when(z < n_seq - 1 if way == 0 else z > 0)
                    def _():
                        along(w, owner, way).wait_send()


def keys_and_values(database, w_key, w_value):
    n_seq, n_head = lax.axis_size("seq"), lax.axis_size("head")
    rows, feats = database.shape
    depth, width = w_key.shape
    vmem = pl.BlockSpec(memory_space=pltpu.VMEM)
    return pl.pallas_call(
        functools.partial(project_kernel, n_seq, n_head),
        out_shape=[jax.ShapeDtypeStruct((rows, width), jnp.bfloat16)] * 2,
        in_specs=[pl.BlockSpec(memory_space=pl.ANY), vmem, vmem],
        out_specs=[vmem, vmem],
        scratch_shapes=[
            pltpu.VMEM((rows, feats * n_head), jnp.bfloat16),
            pltpu.VMEM((2, depth * n_seq, width), jnp.bfloat16),
            pltpu.VMEM((2, rows, width), jnp.float32),
            pltpu.SemaphoreType.DMA((2, n_seq, 2)),
            pltpu.SemaphoreType.DMA((2, n_seq)),
            pltpu.SemaphoreType.DMA((2, n_seq)),
            pltpu.SemaphoreType.DMA((2, n_seq)),
            pltpu.SemaphoreType.DMA((n_head,)),
            pltpu.SemaphoreType.DMA((n_head,)),
            pltpu.SemaphoreType.DMA,
        ],
        compiler_params=pltpu.CompilerParams(
            collective_id=0, has_side_effects=True, vmem_limit_bytes=56 * 1024 * 1024
        ),
        cost_estimate=pl.CostEstimate(
            flops=4 * rows * depth * n_seq * width,
            bytes_accessed=500 * 1024 * 1024,
            transcendentals=0,
        ),
    )(database, w_key, w_value)


def local(tokens, norm_gain, w_query, w_key, w_value, w_out, database, nbr_shard, nbr_row):
    rows_dev, ntok, feat_dev = database.shape
    part = partial_query(normalize(tokens, norm_gain), w_query)
    part, w_key, w_value = lax.optimization_barrier((part, w_key, w_value))
    query = whole_query(part)
    keys, values = keys_and_values(database.reshape(rows_dev * ntok, feat_dev), w_key, w_value)
    keys, values, w_out = lax.optimization_barrier((keys, values, w_out))
    out_halves = gather_halves(w_out)

    me = lax.axis_index("seq")
    near = lax.all_gather(jnp.concatenate([nbr_shard, nbr_row], axis=1), "seq", axis=0, tiled=True)
    here = near[:, :2] == me
    mine = jnp.any(here, axis=1)
    row = jnp.sum(jnp.where(here, near[:, 2:], 0), axis=1)

    spans = near.shape[0]
    width = w_key.shape[1]
    heads_dev = width // HD
    span_len = query.shape[0] // spans
    keys = keys.reshape(rows_dev, ntok, width)
    values = values.reshape(rows_dev, ntok, width)
    keys = jnp.take(keys, row, axis=0).reshape(spans, ntok, heads_dev, HD)
    values = jnp.take(values, row, axis=0).reshape(spans, ntok, heads_dev, HD)
    qh = query.reshape(spans, span_len, heads_dev, HD)
    scores = jnp.einsum("cqhd,ckhd->chqk", qh, keys, preferred_element_type=jnp.float32)
    scores = jnp.where(mine[:, None, None, None], scores, -jnp.inf)
    top = jnp.max(scores, axis=-1)
    summed = jnp.sum(jnp.exp(scores - jnp.where(jnp.isfinite(top), top, 0.0)[..., None]), axis=-1)
    tops, sums = lax.all_gather(jnp.stack([top, summed]), "seq", axis=1)
    most = jnp.max(tops, axis=0)
    denominator = jnp.sum(jnp.exp(tops - most) * sums, axis=0)
    weights = (jnp.exp(scores - most[..., None]) / denominator[..., None]).astype(jnp.bfloat16)
    context = jnp.einsum("chqk,ckhd->cqhd", weights, values, preferred_element_type=jnp.float32)
    context = context.astype(jnp.bfloat16).reshape(spans * span_len, width)
    context = lax.psum_scatter(context, "seq", scatter_dimension=0, tiled=True)
    attended = project(lax.all_gather(context, "head", axis=1, tiled=True), out_halves)
    return attended.astype(jnp.bfloat16)


def solution(mesh):
    return jax.shard_map(
        local,
        mesh=mesh,
        in_specs=(
            P(("groups", "seq"), "head"),
            P(),
            P("seq", "head"),
            P("seq", "head"),
            P("seq", "head"),
            P("seq", "head"),
            P(("groups", "seq"), None, "head"),
            P(("groups", "seq"), None),
            P(("groups", "seq"), None),
        ),
        out_specs=P(("groups", "seq"), "head"),
        check_vma=False,
    )
```

```python
import functools

import jax
import jax.numpy as jnp
from jax import lax
from jax.experimental import pallas as pl
from jax.experimental.pallas import tpu as pltpu
from jax.sharding import PartitionSpec as P

HD = 128


def shifted(pieces, axis):
    num, me = lax.axis_size(axis), lax.axis_index(axis)
    got = [pieces(0)]
    for k in range(1, num):
        got.append(lax.ppermute(pieces(k), axis, [(i, (i + k) % num) for i in range(num)]))
    return got, lax.rem(me - jnp.arange(num) + num, num)


def project(rows, halves):
    mine, other = (jnp.dot(rows, half, preferred_element_type=jnp.float32) for half in halves)
    first = lax.axis_index("groups") == 0
    return jnp.concatenate([jnp.where(first, mine, other), jnp.where(first, other, mine)], axis=1)


def normalize(tokens, norm_gain):
    x = tokens.astype(jnp.float32)
    feat_dev = tokens.shape[1]
    total = lax.psum(jnp.sum(x * x, axis=-1, keepdims=True), "head")
    inverse = lax.rsqrt(total / (feat_dev * lax.axis_size("head")) + 1e-06)
    gain = lax.dynamic_slice_in_dim(norm_gain, lax.axis_index("head") * feat_dev, feat_dev)
    return (x * inverse * gain).astype(jnp.bfloat16)


def partial_query(normed, w_query):
    scale = jnp.sqrt(jnp.float32(HD))
    num = lax.axis_size("seq")
    if num == lax.axis_size("head"):
        swap = [(a * num + b, b * num + a) for a in range(num) for b in range(num)]
        turned = lax.ppermute(normed, ("seq", "head"), swap)
        got, order = shifted(lambda k: turned, "head")
        rows = jnp.concatenate(got, axis=0)
        part = jnp.dot(rows, w_query, preferred_element_type=jnp.float32) / scale
        return part.astype(jnp.bfloat16), order
    rows = lax.all_gather(normed, "head", axis=1, tiled=True)
    query = jnp.dot(
        rows,
        lax.all_gather(w_query, "seq", axis=0, tiled=True),
        preferred_element_type=jnp.float32,
    )
    return (query / scale).astype(jnp.bfloat16), None


def whole_query(part, order):
    if order is not None:
        query = lax.psum(part, "seq").reshape(order.shape[0], -1, part.shape[1])
        return jnp.take(query, order, axis=0).reshape(part.shape)
    return lax.all_gather(part, "seq", axis=0, tiled=True)


MESH = pl.DeviceIdType.MESH


def project_kernel(
    n_seq, n_head, database, w_key, w_value, w_out, keys, values, out_half, whole, held, total,
    near_send, near_recv, side_send, side_recv, row_send, row_recv, row_copy, out_copy,
):
    g, z, h = lax.axis_index("groups"), lax.axis_index("seq"), lax.axis_index("head")
    weights = (w_key, w_value)
    depth, width = w_key.shape
    half = depth // 2
    feats = database.shape[1]
    tile = min(256, width)

    barrier = pltpu.get_barrier_semaphore()

    def greet(**where):
        pl.semaphore_signal(barrier, inc=1, device_id=where, device_id_type=MESH)

    @pl.when(z > 0)
    def _():
        greet(seq=z - 1)

    @pl.when(z < n_seq - 1)
    def _():
        greet(seq=z + 1)

    greet(groups=1 - g)
    for step in range(1, n_head):
        greet(head=lax.rem(h + step, n_head))

    ends = jnp.where(z > 0, 0, 1) + jnp.where(z < n_seq - 1, 0, 1)
    pl.semaphore_wait(barrier, n_head + 2 - ends)

    def span(owner, part):
        return pl.ds(pl.multiple_of(owner * depth + part * half, half), half)

    def along(w, owner, way, own=False):
        source = held.at[w, span(owner, g)]
        if own:
            source = weights[w].at[pl.ds(pl.multiple_of(g * half, half), half)]
        return pltpu.make_async_remote_copy(
            src_ref=source,
            dst_ref=held.at[w, span(owner, g)],
            send_sem=near_send.at[w, owner, way],
            recv_sem=near_recv.at[w, owner],
            device_id={"seq": z + 1 - 2 * way},
            device_id_type=MESH,
        )

    def across(w, owner, part):
        return pltpu.make_async_remote_copy(
            src_ref=held.at[w, span(owner, part)],
            dst_ref=held.at[w, span(owner, part)],
            send_sem=side_send.at[w, owner],
            recv_sem=side_recv.at[w, owner],
            device_id={"groups": 1 - g},
            device_id_type=MESH,
        )

    def columns(source):
        return pl.ds(pl.multiple_of(source * feats, feats), feats)

    def row_move(source, target):
        return pltpu.make_async_remote_copy(
            src_ref=database,
            dst_ref=whole.at[:, columns(source)],
            send_sem=row_send.at[target],
            recv_sem=row_recv.at[source],
            device_id={"head": target},
            device_id_type=MESH,
        )

    for w in range(2):

        @pl.when(z < n_seq - 1)
        def _():
            along(w, z, 0, own=True).start()

        @pl.when(z > 0)
        def _():
            along(w, z, 1, own=True).start()

    for step in range(1, n_head):
        row_move(h, lax.rem(h + step, n_head)).start()
    keep = pltpu.make_async_copy(database, whole.at[:, columns(h)], row_copy)
    keep.start()
    out_cols = out_half.shape[1]
    chosen = w_out.at[:, pl.ds(pl.multiple_of(g * out_cols, out_cols), out_cols)]
    hand_on = pltpu.make_async_copy(chosen, out_half, out_copy)
    hand_on.start()

    def valid(d, way):
        return z - d >= 0 if way == 0 else z + d < n_seq

    def owner_of(d, way):
        return z - d if way == 0 else z + d

    def forward(d):
        for w in range(2):
            for way in range(2):
                owner = owner_of(d, way)

                @pl.when(valid(d, way))
                def _():
                    along(w, owner, way).wait_recv()
                    across(w, owner, g).start()

                    @pl.when(z < n_seq - 1 if way == 0 else z > 0)
                    def _():
                        along(w, owner, way).start()

    def add(w, owner, block, first=False):
        left = whole.at[:, pl.ds(pl.multiple_of(owner * depth, depth), depth)]

        def body(t, carry):
            at = pl.ds(pl.multiple_of(t * tile, tile), tile)
            term = jnp.dot(left[...], block[:, at], preferred_element_type=jnp.float32)
            if first:
                total[w, :, at] = term
            else:
                total[w, :, at] += term
            return carry

        lax.fori_loop(0, width // tile, body, 0)

    def multiply(d):
        for w in range(2):
            for way in range(2):
                owner = owner_of(d, way)

                @pl.when(valid(d, way))
                def _():
                    across(w, owner, 1 - g).wait_recv()
                    add(w, owner, held.at[w, pl.ds(pl.multiple_of(owner * depth, depth), depth)])

    early = min(2, n_seq - 1)
    for d in range(1, early + 1):
        forward(d)
    keep.wait()
    for step in range(1, n_head):
        source = lax.rem(h + step, n_head)
        row_move(source, source).wait_recv()
    for w in range(2):
        add(w, z, weights[w], first=True)
    for d in range(1, n_seq):
        if d > early:
            forward(d)
        if d < n_seq - 1:
            multiply(d)
    if n_seq > 1:
        multiply(n_seq - 1)

    for i in range(width // HD):
        keys[i] = total[0, :, i * HD : (i + 1) * HD].astype(keys.dtype)
        values[i] = total[1, :, i * HD : (i + 1) * HD].astype(values.dtype)
    hand_on.wait()

    for step in range(1, n_head):
        row_move(h, lax.rem(h + step, n_head)).wait_send()
    for w in range(2):

        @pl.when(z < n_seq - 1)
        def _():
            along(w, z, 0, own=True).wait_send()

        @pl.when(z > 0)
        def _():
            along(w, z, 1, own=True).wait_send()

        for d in range(1, n_seq):
            for way in range(2):
                owner = owner_of(d, way)

                @pl.when(valid(d, way))
                def _():
                    across(w, owner, g).wait_send()

                    @pl.when(z < n_seq - 1 if way == 0 else z > 0)
                    def _():
                        along(w, owner, way).wait_send()


def keys_and_values(database, w_key, w_value, w_out):
    n_seq, n_head = lax.axis_size("seq"), lax.axis_size("head")
    rows, feats = database.shape
    depth, width = w_key.shape
    vmem = pl.BlockSpec(memory_space=pltpu.VMEM)
    return pl.pallas_call(
        functools.partial(project_kernel, n_seq, n_head),
        out_shape=[jax.ShapeDtypeStruct((width // HD, rows, HD), jnp.bfloat16)] * 2
        + [jax.ShapeDtypeStruct((w_out.shape[0], w_out.shape[1] // 2), jnp.bfloat16)],
        in_specs=[pl.BlockSpec(memory_space=pl.ANY), vmem, vmem, pl.BlockSpec(memory_space=pl.ANY)],
        out_specs=[vmem, vmem, pl.BlockSpec(memory_space=pl.ANY)],
        scratch_shapes=[
            pltpu.VMEM((rows, feats * n_head), jnp.bfloat16),
            pltpu.VMEM((2, depth * n_seq, width), jnp.bfloat16),
            pltpu.VMEM((2, rows, width), jnp.float32),
            pltpu.SemaphoreType.DMA((2, n_seq, 2)),
            pltpu.SemaphoreType.DMA((2, n_seq)),
            pltpu.SemaphoreType.DMA((2, n_seq)),
            pltpu.SemaphoreType.DMA((2, n_seq)),
            pltpu.SemaphoreType.DMA((n_head,)),
            pltpu.SemaphoreType.DMA((n_head,)),
            pltpu.SemaphoreType.DMA,
            pltpu.SemaphoreType.DMA,
        ],
        compiler_params=pltpu.CompilerParams(
            collective_id=0, has_side_effects=True, vmem_limit_bytes=56 * 1024 * 1024
        ),
        cost_estimate=pl.CostEstimate(
            flops=4 * rows * depth * n_seq * width,
            bytes_accessed=500 * 1024 * 1024,
            transcendentals=0,
        ),
    )(database, w_key, w_value, w_out)


def local(tokens, norm_gain, w_query, w_key, w_value, w_out, database, nbr_shard, nbr_row):
    rows_dev, ntok, feat_dev = database.shape
    part, order = partial_query(normalize(tokens, norm_gain), w_query)
    own = jnp.concatenate([nbr_shard, nbr_row], axis=1)
    got, by_seq = shifted(lambda k: own, "seq")
    near = jnp.take(jnp.stack(got), by_seq, axis=0).reshape(-1, 4)
    part, w_key, w_value = lax.optimization_barrier((part, w_key, w_value))
    query = whole_query(part, order)
    flat = database.reshape(rows_dev * ntok, feat_dev)
    keys, values, out_half = keys_and_values(flat, w_key, w_value, w_out)
    out_mine = lax.all_gather(out_half, "seq", axis=0, tiled=True)
    out_halves = out_mine, lax.ppermute(out_mine, "groups", [(0, 1), (1, 0)])

    num, me = lax.axis_size("seq"), lax.axis_index("seq")
    here = near[:, :2] == me
    mine = jnp.any(here, axis=1)
    row = jnp.sum(jnp.where(here, near[:, 2:], 0), axis=1)
    spans = near.shape[0]
    spans_dev = spans // num
    width = w_key.shape[1]
    heads_dev = width // HD
    span_len = query.shape[0] // spans
    keys = jnp.take(keys.reshape(heads_dev, rows_dev, ntok, HD), row, axis=1)
    values = jnp.take(values.reshape(heads_dev, rows_dev, ntok, HD), row, axis=1)
    qh = query.reshape(spans, span_len, heads_dev, HD).transpose(2, 0, 1, 3)
    scores = jnp.einsum("hcqd,hckd->hcqk", qh, keys, preferred_element_type=jnp.float32)
    top = jnp.max(scores, axis=-1, keepdims=True)
    raised = jnp.exp(scores - top)
    summed = jnp.sum(raised, axis=-1, keepdims=True)
    weights = (raised / summed).astype(jnp.bfloat16)
    context = jnp.einsum("hcqk,hckd->hcqd", weights, values, preferred_element_type=jnp.float32)
    context = context.astype(jnp.bfloat16)
    top = jnp.where(mine[:, None], top[..., 0], -jnp.inf)
    stats = jnp.stack([top, summed[..., 0]])

    def for_device(array, axis):
        def piece(k):
            start = lax.rem(me + k, num) * spans_dev
            return lax.dynamic_slice_in_dim(array, start, spans_dev, axis=axis)

        return piece

    stats = jnp.stack(shifted(for_device(stats, 2), "seq")[0])
    tops, sums = stats[:, 0], stats[:, 1]
    shares = jnp.exp(tops - jnp.max(tops, axis=0)) * sums
    shares = shares / jnp.sum(shares, axis=0)
    pieces = shifted(for_device(context, 1), "seq")[0]
    context = sum(shares[i][..., None] * piece.astype(jnp.float32) for i, piece in enumerate(pieces))
    context = context.astype(jnp.bfloat16).transpose(1, 2, 0, 3).reshape(spans_dev * span_len, width)
    attended = project(lax.all_gather(context, "head", axis=1, tiled=True), out_halves)
    return attended.astype(jnp.bfloat16)


def solution(mesh):
    return jax.shard_map(
        local,
        mesh=mesh,
        in_specs=(
            P(("groups", "seq"), "head"),
            P(),
            P("seq", "head"),
            P("seq", "head"),
            P("seq", "head"),
            P("seq", "head"),
            P(("groups", "seq"), None, "head"),
            P(("groups", "seq"), None),
            P(("groups", "seq"), None),
        ),
        out_specs=P(("groups", "seq"), "head"),
        check_vma=False,
    )
```

```python
import functools

import jax
import jax.numpy as jnp
from jax import lax
from jax.experimental import pallas as pl
from jax.experimental.pallas import tpu as pltpu
from jax.sharding import PartitionSpec as P

HD = 128


def shifted(pieces, axis):
    num, me = lax.axis_size(axis), lax.axis_index(axis)
    got = [pieces(0)]
    for k in range(1, num):
        got.append(lax.ppermute(pieces(k), axis, [(i, (i + k) % num) for i in range(num)]))
    return got, lax.rem(me - jnp.arange(num) + num, num)


def normalize(tokens, norm_gain):
    x = tokens.astype(jnp.float32)
    feat_dev = tokens.shape[1]
    total = lax.psum(jnp.sum(x * x, axis=-1, keepdims=True), "head")
    inverse = lax.rsqrt(total / (feat_dev * lax.axis_size("head")) + 1e-06)
    gain = lax.dynamic_slice_in_dim(norm_gain, lax.axis_index("head") * feat_dev, feat_dev)
    return (x * inverse * gain).astype(jnp.bfloat16)


def partial_query(normed, w_query):
    scale = jnp.sqrt(jnp.float32(HD))
    num = lax.axis_size("seq")
    if num == lax.axis_size("head"):
        swap = [(a * num + b, b * num + a) for a in range(num) for b in range(num)]
        turned = lax.ppermute(normed, ("seq", "head"), swap)
        got, order = shifted(lambda k: turned, "head")
        rows = jnp.concatenate(got, axis=0)
        part = jnp.dot(rows, w_query, preferred_element_type=jnp.float32) / scale
        return part.astype(jnp.bfloat16), order
    rows = lax.all_gather(normed, "head", axis=1, tiled=True)
    query = jnp.dot(
        rows,
        lax.all_gather(w_query, "seq", axis=0, tiled=True),
        preferred_element_type=jnp.float32,
    )
    return (query / scale).astype(jnp.bfloat16), None


def whole_query(part, order):
    if order is not None:
        query = lax.psum(part, "seq").reshape(order.shape[0], -1, part.shape[1])
        return jnp.take(query, order, axis=0).reshape(part.shape)
    return lax.all_gather(part, "seq", axis=0, tiled=True)


MESH = pl.DeviceIdType.MESH


def project_kernel(
    n_seq, n_head, database, w_key, w_value, keys, values, whole, held, total,
    near_send, near_recv, side_send, side_recv, row_send, row_recv, row_copy,
):
    g, z, h = lax.axis_index("groups"), lax.axis_index("seq"), lax.axis_index("head")
    weights = (w_key, w_value)
    depth, width = w_key.shape
    half = depth // 2
    feats = database.shape[1]
    tile = min(256, width)

    barrier = pltpu.get_barrier_semaphore()

    def greet(**where):
        pl.semaphore_signal(barrier, inc=1, device_id=where, device_id_type=MESH)

    @pl.when(z > 0)
    def _():
        greet(seq=z - 1)

    @pl.when(z < n_seq - 1)
    def _():
        greet(seq=z + 1)

    greet(groups=1 - g)
    for step in range(1, n_head):
        greet(head=lax.rem(h + step, n_head))

    ends = jnp.where(z > 0, 0, 1) + jnp.where(z < n_seq - 1, 0, 1)
    pl.semaphore_wait(barrier, n_head + 2 - ends)

    def span(owner, part):
        return pl.ds(pl.multiple_of(owner * depth + part * half, half), half)

    def along(w, owner, way, own=False):
        source = held.at[w, span(owner, g)]
        if own:
            source = weights[w].at[pl.ds(pl.multiple_of(g * half, half), half)]
        return pltpu.make_async_remote_copy(
            src_ref=source,
            dst_ref=held.at[w, span(owner, g)],
            send_sem=near_send.at[w, owner, way],
            recv_sem=near_recv.at[w, owner],
            device_id={"seq": z + 1 - 2 * way},
            device_id_type=MESH,
        )

    def across(w, owner, part):
        return pltpu.make_async_remote_copy(
            src_ref=held.at[w, span(owner, part)],
            dst_ref=held.at[w, span(owner, part)],
            send_sem=side_send.at[w, owner],
            recv_sem=side_recv.at[w, owner],
            device_id={"groups": 1 - g},
            device_id_type=MESH,
        )

    def columns(source):
        return pl.ds(pl.multiple_of(source * feats, feats), feats)

    def row_move(source, target):
        return pltpu.make_async_remote_copy(
            src_ref=database,
            dst_ref=whole.at[:, columns(source)],
            send_sem=row_send.at[target],
            recv_sem=row_recv.at[source],
            device_id={"head": target},
            device_id_type=MESH,
        )

    for w in range(2):

        @pl.when(z < n_seq - 1)
        def _():
            along(w, z, 0, own=True).start()

        @pl.when(z > 0)
        def _():
            along(w, z, 1, own=True).start()

    for step in range(1, n_head):
        row_move(h, lax.rem(h + step, n_head)).start()
    keep = pltpu.make_async_copy(database, whole.at[:, columns(h)], row_copy)
    keep.start()

    def valid(d, way):
        return z - d >= 0 if way == 0 else z + d < n_seq

    def owner_of(d, way):
        return z - d if way == 0 else z + d

    def forward(d):
        for w in range(2):
            for way in range(2):
                owner = owner_of(d, way)

                @pl.when(valid(d, way))
                def _():
                    along(w, owner, way).wait_recv()
                    across(w, owner, g).start()

                    @pl.when(z < n_seq - 1 if way == 0 else z > 0)
                    def _():
                        along(w, owner, way).start()

    def add(w, owner, block, first=False):
        left = whole.at[:, pl.ds(pl.multiple_of(owner * depth, depth), depth)]

        def body(t, carry):
            at = pl.ds(pl.multiple_of(t * tile, tile), tile)
            term = jnp.dot(left[...], block[:, at], preferred_element_type=jnp.float32)
            if first:
                total[w, :, at] = term
            else:
                total[w, :, at] += term
            return carry

        lax.fori_loop(0, width // tile, body, 0)

    def multiply(d):
        for w in range(2):
            for way in range(2):
                owner = owner_of(d, way)

                @pl.when(valid(d, way))
                def _():
                    across(w, owner, 1 - g).wait_recv()
                    add(w, owner, held.at[w, pl.ds(pl.multiple_of(owner * depth, depth), depth)])

    early = min(2, n_seq - 1)
    for d in range(1, early + 1):
        forward(d)
    keep.wait()
    for step in range(1, n_head):
        source = lax.rem(h + step, n_head)
        row_move(source, source).wait_recv()
    for w in range(2):
        add(w, z, weights[w], first=True)
    for d in range(1, n_seq):
        if d > early:
            forward(d)
        if d < n_seq - 1:
            multiply(d)
    if n_seq > 1:
        multiply(n_seq - 1)

    for i in range(width // HD):
        keys[i] = total[0, :, i * HD : (i + 1) * HD].astype(keys.dtype)
        values[i] = total[1, :, i * HD : (i + 1) * HD].astype(values.dtype)

    for step in range(1, n_head):
        row_move(h, lax.rem(h + step, n_head)).wait_send()
    for w in range(2):

        @pl.when(z < n_seq - 1)
        def _():
            along(w, z, 0, own=True).wait_send()

        @pl.when(z > 0)
        def _():
            along(w, z, 1, own=True).wait_send()

        for d in range(1, n_seq):
            for way in range(2):
                owner = owner_of(d, way)

                @pl.when(valid(d, way))
                def _():
                    across(w, owner, g).wait_send()

                    @pl.when(z < n_seq - 1 if way == 0 else z > 0)
                    def _():
                        along(w, owner, way).wait_send()


def keys_and_values(database, w_key, w_value):
    n_seq, n_head = lax.axis_size("seq"), lax.axis_size("head")
    rows, feats = database.shape
    depth, width = w_key.shape
    vmem = pl.BlockSpec(memory_space=pltpu.VMEM)
    return pl.pallas_call(
        functools.partial(project_kernel, n_seq, n_head),
        out_shape=[jax.ShapeDtypeStruct((width // HD, rows, HD), jnp.bfloat16)] * 2,
        in_specs=[pl.BlockSpec(memory_space=pl.ANY), vmem, vmem],
        out_specs=[vmem, vmem],
        scratch_shapes=[
            pltpu.VMEM((rows, feats * n_head), jnp.bfloat16),
            pltpu.VMEM((2, depth * n_seq, width), jnp.bfloat16),
            pltpu.VMEM((2, rows, width), jnp.float32),
            pltpu.SemaphoreType.DMA((2, n_seq, 2)),
            pltpu.SemaphoreType.DMA((2, n_seq)),
            pltpu.SemaphoreType.DMA((2, n_seq)),
            pltpu.SemaphoreType.DMA((2, n_seq)),
            pltpu.SemaphoreType.DMA((n_head,)),
            pltpu.SemaphoreType.DMA((n_head,)),
            pltpu.SemaphoreType.DMA,
        ],
        compiler_params=pltpu.CompilerParams(
            collective_id=0, has_side_effects=True, vmem_limit_bytes=56 * 1024 * 1024
        ),
        cost_estimate=pl.CostEstimate(
            flops=4 * rows * depth * n_seq * width,
            bytes_accessed=500 * 1024 * 1024,
            transcendentals=0,
        ),
    )(database, w_key, w_value)


def local(tokens, norm_gain, w_query, w_key, w_value, w_out, database, nbr_shard, nbr_row):
    rows_dev, ntok, feat_dev = database.shape
    part, order = partial_query(normalize(tokens, norm_gain), w_query)
    own = jnp.concatenate([nbr_shard, nbr_row], axis=1)
    got, by_seq = shifted(lambda k: own, "seq")
    near = jnp.take(jnp.stack(got), by_seq, axis=0).reshape(-1, 4)
    part, w_key, w_value = lax.optimization_barrier((part, w_key, w_value))
    query = whole_query(part, order)
    flat = database.reshape(rows_dev * ntok, feat_dev)
    keys, values = keys_and_values(flat, w_key, w_value)
    cols = w_out.shape[1] // 2
    part_of = lax.axis_index("groups")
    chosen = lax.dynamic_slice_in_dim(w_out, part_of * cols, cols, axis=1)
    out_mine = lax.all_gather(chosen, "seq", axis=0, tiled=True)

    num, me = lax.axis_size("seq"), lax.axis_index("seq")
    here = near[:, :2] == me
    mine = jnp.any(here, axis=1)
    row = jnp.sum(jnp.where(here, near[:, 2:], 0), axis=1)
    spans = near.shape[0]
    spans_dev = spans // num
    width = w_key.shape[1]
    heads_dev = width // HD
    span_len = query.shape[0] // spans
    keys = jnp.take(keys.reshape(heads_dev, rows_dev, ntok, HD), row, axis=1)
    values = jnp.take(values.reshape(heads_dev, rows_dev, ntok, HD), row, axis=1)
    qh = query.reshape(spans, span_len, heads_dev, HD).transpose(2, 0, 1, 3)
    scores = jnp.einsum("hcqd,hckd->hcqk", qh, keys, preferred_element_type=jnp.float32)
    top = jnp.max(scores, axis=-1, keepdims=True)
    raised = jnp.exp(scores - top)
    summed = jnp.sum(raised, axis=-1, keepdims=True)
    weights = (raised / summed).astype(jnp.bfloat16)
    context = jnp.einsum("hcqk,hckd->hcqd", weights, values, preferred_element_type=jnp.float32)
    context = context.astype(jnp.bfloat16)
    top = jnp.where(mine[:, None], top[..., 0], -jnp.inf)
    stats = jnp.stack([top, summed[..., 0]])

    def for_device(array, axis):
        def piece(k):
            start = lax.rem(me + k, num) * spans_dev
            return lax.dynamic_slice_in_dim(array, start, spans_dev, axis=axis)

        return piece

    stats = jnp.stack(shifted(for_device(stats, 2), "seq")[0])
    tops, sums = stats[:, 0], stats[:, 1]
    shares = jnp.exp(tops - jnp.max(tops, axis=0)) * sums
    shares = shares / jnp.sum(shares, axis=0)
    pieces = shifted(for_device(context, 1), "seq")[0]
    context = sum(shares[i][..., None] * piece.astype(jnp.float32) for i, piece in enumerate(pieces))
    context = context.astype(jnp.bfloat16).transpose(1, 2, 0, 3).reshape(spans_dev * span_len, width)
    whole = lax.all_gather(context, "head", axis=1, tiled=True)
    depth = w_out.shape[0]
    left = lax.dynamic_slice_in_dim(w_out, (1 - part_of) * cols, cols, axis=1)
    other = 0.0
    for k in range(num):
        start = lax.rem(me + k, num) * depth
        if k > 0:
            block = lax.dynamic_slice_in_dim(out_mine, start, depth, axis=0)
            left = lax.ppermute(block, "groups", [(0, 1), (1, 0)])
        rows = lax.dynamic_slice_in_dim(whole, start, depth, axis=1)
        other = other + jnp.dot(rows, left, preferred_element_type=jnp.float32)
    mine = jnp.dot(whole, out_mine, preferred_element_type=jnp.float32)
    first = part_of == 0
    attended = jnp.concatenate([jnp.where(first, mine, other), jnp.where(first, other, mine)], axis=1)
    return attended.astype(jnp.bfloat16)


def solution(mesh):
    return jax.shard_map(
        local,
        mesh=mesh,
        in_specs=(
            P(("groups", "seq"), "head"),
            P(),
            P("seq", "head"),
            P("seq", "head"),
            P("seq", "head"),
            P("seq", "head"),
            P(("groups", "seq"), None, "head"),
            P(("groups", "seq"), None),
            P(("groups", "seq"), None),
        ),
        out_specs=P(("groups", "seq"), "head"),
        check_vma=False,
    )
```
